32 devices in a mesh: groups: 2 (over y), blk: 4 (over z), inner: 4 (over x, core).
Axes of the slice: x: 2, y: 2, z: 4, core: 2. Of those that a mesh axis runs over, the one named last changes fastest.
Arguments:
- points: float32 [8192, 64], P(('groups', 'blk', 'inner')), parts along dimension 0, may hold values from -6 to 6
- inverse_scale: float32 [128], P('groups'), parts along dimension 0, may hold values from 0.125 to 0.375
- noise_var: float32 [8192], P(('groups', 'blk', 'inner')), parts along dimension 0, may hold values from 0.1 to 1
- solution: float32 [8192, 32], P(('groups', 'blk', 'inner')), parts along dimension 0, may hold values from -6 to 6
- residual: float32 [8192, 32], P(('groups', 'blk', 'inner')), parts along dimension 0, may hold values from -6 to 6
- direction: float32 [8192, 32], P(('groups', 'blk', 'inner')), parts along dimension 0, may hold values from -6 to 6
Outputs:
- solution_next: float32 [8192, 32], P(('groups', 'blk', 'inner')), parts along dimension 0
- residual_next: float32 [8192, 32], P(('groups', 'blk', 'inner')), parts along dimension 0
- direction_next: float32 [8192, 32], P(('groups', 'blk', 'inner')), parts along dimension 0
The draws below stay inside these ranges and needn't reach their ends.
There are 2 independent parts, one for each index of `groups`. The reference program is written for one: setup_inputs(seed, part) draws one part's arguments, and reference() takes and returns one part's arrays. A program takes and returns all parts, laid end to end along the dimension named above; each array names one. Nothing has to cross between parts.
All inputs are finite; a program needn't handle non-finite values.
Results may differ from the reference program's by a relative error of at most 0.0003.
Values sent between devices are 32-bit elements; how exact they have to be, the bound alone decides.
A program may use at most 64 MiB of HBM per device.

```python
import math
import jax
import jax.numpy as jnp
from jax import lax

F = 64
S = 32
POINTS = 4096


def block_levels(stream_key, shape, cuts, least, high):
    level = 1.0
    for dim, parts in cuts:
        heights = jax.random.uniform(jax.random.fold_in(jax.random.fold_in(stream_key, 6), dim), (parts,), jnp.float32, least / len(cuts), high / len(cuts))
        level = level * jnp.repeat(jnp.exp(heights), shape[dim] // parts).reshape((-1,) + (1,) * (len(shape) - 1 - dim))
    return level


def normal_values(own_key, extent, spread, bound, split=(), held_as=jnp.bfloat16):
    entries = jax.random.normal(own_key, extent, jnp.float32) * spread
    if len(split) > 0:
        entries = block_levels(own_key, extent, split, -0.22, 0.18) * entries
    return jnp.clip(entries, min=-bound, max=bound).astype(held_as)


def setup_inputs(seed: int = 0, part: int = 0) -> dict:
    streams_of = jax.random.split(jax.random.key(seed), 7)
    own_keys = jax.random.split(jax.random.fold_in(streams_of[6], part), 7)
    return {
        "points": normal_values(own_keys[0], (POINTS, F), 1.0, 6.0, ((0, 16),), jnp.float32),
        "inverse_scale": jnp.clip(jnp.exp(jax.random.uniform(own_keys[1], (F,), jnp.float32, math.log(0.125), math.log(0.375))), 0.125, 0.375),
        "noise_var": jnp.clip(jnp.exp(math.log(1.0) - 2.3025851 * jax.random.uniform(own_keys[2], (POINTS,), jnp.float32) ** block_levels(own_keys[2], (POINTS,), ((0, 16),), -0.2, 0.2)), 0.1, 1.0),
        "solution": normal_values(own_keys[3], (POINTS, S), 1.0, 6.0, ((0, 16),), jnp.float32),
        "residual": normal_values(own_keys[4], (POINTS, S), 1.0, 6.0, ((0, 16),), jnp.float32),
        "direction": normal_values(own_keys[5], (POINTS, S), 1.0, 6.0, ((0, 16),), jnp.float32),
    }


def matern(sq):
    root = jnp.sqrt(5.0 * jnp.maximum(sq, 0.0))
    return (1.0 + root + root * root / 3.0) * jnp.exp(-root)

def reference(points, inverse_scale, noise_var, solution, residual, direction):
    high = lax.Precision.HIGHEST
    scaled = points * inverse_scale
    norms = lax.optimization_barrier(jnp.sum(scaled * scaled, axis=1))
    blocks = POINTS // 512 if POINTS % 512 == 0 else POINTS
    width = POINTS // blocks
    row_blocks = scaled.reshape(blocks, width, F)
    norm_blocks = norms.reshape(blocks, width)

    def one_block(pair):
        rows_z, rows_n = pair
        cross = jnp.dot(rows_z, scaled.T, precision=high)
        sq = rows_n[:, None] + norms[None, :] - 2.0 * cross
        return jnp.dot(matern(sq), direction, precision=high)
    image = lax.map(one_block, (row_blocks, norm_blocks)).reshape(POINTS, S)
    image = image + noise_var[:, None] * direction
    curv = jnp.dot(direction.T, image, precision=high)
    gram = jnp.dot(residual.T, residual, precision=high)
    alpha = jax.scipy.linalg.cho_solve((jnp.linalg.cholesky(curv), True), gram)
    solution_next = solution + jnp.dot(direction, alpha, precision=high)
    residual_next = residual - jnp.dot(image, alpha, precision=high)
    gram_next = jnp.dot(residual_next.T, residual_next, precision=high)
    beta = jax.scipy.linalg.cho_solve((jnp.linalg.cholesky(gram), True), gram_next)
    direction_next = residual_next + jnp.dot(direction, beta, precision=high)
    return (solution_next, residual_next, direction_next)
```

```python
import functools
import math

import jax
import jax.numpy as jnp
from jax import lax
from jax.experimental import pallas as pl
from jax.experimental.pallas import tpu as pltpu
from jax.sharding import PartitionSpec as P

MESH = pl.DeviceIdType.MESH
HIGH = lax.Precision.HIGHEST
LN2 = math.log(2.0)
FEATURE_SCALE = math.sqrt(5.0) / LN2
f32 = jnp.float32
bf16 = jnp.bfloat16


def dot(a, b, ca, cb, precision=HIGH):
    return lax.dot_general(a, b, (((ca,), (cb,)), ((), ())), precision=precision, preferred_element_type=f32)


def lanes(shape):
    return lax.broadcasted_iota(jnp.int32, shape, len(shape) - 1)


def halves(packed):
    hi = packed.astype(bf16).astype(f32)
    lo = (packed - hi).astype(bf16).astype(f32)
    return hi, lo


def row_operand(packed):
    hi, lo = halves(packed)
    left = lanes(packed.shape) < 64
    lo_r = pltpu.roll(lo, 64, 1)
    top = jnp.where(left, hi, lo_r) * -2.0
    low = jnp.where(left, lo_r, hi) * -2.0
    both = jnp.concatenate([top, low], axis=0).astype(bf16)
    sq = (hi + lo) * (hi + lo)
    n_top = jnp.sum(jnp.where(left, sq, 0.0), axis=1, keepdims=True)
    n_low = jnp.sum(jnp.where(left, 0.0, sq), axis=1, keepdims=True)
    norms = jnp.concatenate([n_top, n_low], axis=0)
    return jnp.concatenate([both, both], axis=1), norms


def col_operand(packed):
    hi, lo = halves(packed)
    left = lanes(packed.shape) < 64
    hi_r, lo_r = pltpu.roll(hi, 64, 1), pltpu.roll(lo, 64, 1)
    hh = jnp.concatenate([jnp.where(left, hi, hi_r), jnp.where(left, hi_r, hi)], axis=0)
    ll = jnp.concatenate([jnp.where(left, lo, lo_r), jnp.where(left, lo_r, lo)], axis=0)
    sq = (hi + lo) * (hi + lo)
    pick = lanes((8, 128)) < 64
    n_top = dot(jnp.where(pick, 1.0, 0.0), sq, 1, 1)
    n_low = dot(jnp.where(pick, 0.0, 1.0), sq, 1, 1)
    return (
        jnp.concatenate([hh, ll], axis=1).astype(bf16),
        jnp.concatenate([n_top, n_low], axis=1),
    )


def pack4(x):
    n = x.shape[0] // 4
    return jnp.concatenate([x[g * n:(g + 1) * n] for g in range(4)], axis=1)


def unpack4(x):
    return jnp.concatenate([x[:, g * 32:(g + 1) * 32] for g in range(4)], axis=0)


def spread4(packed):
    group = lanes(packed.shape) // 32
    out = []
    for g in range(4):
        m = jnp.where(group == g, packed, 0.0)
        m = m + pltpu.roll(m, 64, 1)
        out.append(m + pltpu.roll(m, 32, 1))
    return jnp.concatenate(out, axis=0)


def dir_operand(packed):
    d = spread4(packed)
    hi, lo = halves(d)
    return jnp.where((lanes(d.shape) // 32) % 2 == 0, hi, lo).astype(bf16)


def eliminate(systems):
    n = systems[0].shape[0]
    rows = lax.broadcasted_iota(jnp.int32, (n, 1), 0)
    for k in range(n):
        done = []
        for a in systems:
            pivot = a[k:k + 1, :] / a[k:k + 1, k:k + 1]
            column = jnp.where(rows == k, 0.0, a[:, k:k + 1])
            done.append(jnp.where(rows == k, pivot, a - column * pivot))
        systems = done
    return [a[:, n:2 * n] for a in systems]


def kernel(nb, ni, points_ref, scale_ref, noise_ref, sol_ref, res_ref, dir_ref, sol_out, res_out, dir_out,
           wrow, cols, a_op, rn, b_op, cn, d_op, acc, parts, sums_i, sums_b,
           w_send, w_recv, c_right, c_left, c_recv, p_send, p_recv, si_send, si_recv, sb_send, sb_recv):
    n = points_ref.shape[0]
    h, q = n // 2, n // 4
    b = lax.axis_index("blk")
    i = lax.axis_index("inner")

    barrier = pltpu.get_barrier_semaphore()
    for off in range(1, ni):
        pl.semaphore_signal(barrier, inc=1, device_id={"inner": lax.rem(i + off, ni)}, device_id_type=MESH)

    @pl.loop(1, nb)
    def _(off):
        pl.semaphore_signal(barrier, inc=1, device_id={"blk": lax.rem(b + off, nb)}, device_id_type=MESH)

    w = points_ref[...] * (scale_ref[...] * FEATURE_SCALE)
    packed_w = jnp.concatenate([w[:h], w[h:]], axis=1)
    wrow[i] = packed_w
    cols[b, :h] = packed_w
    cols[b, h:] = pack4(dir_ref[...])
    pl.semaphore_wait(barrier, ni + nb - 2)

    def w_copy(src, to):
        return pltpu.make_async_remote_copy(
            src_ref=wrow.at[src], dst_ref=wrow.at[src], send_sem=w_send.at[to], recv_sem=w_recv.at[src],
            device_id={"inner": to}, device_id_type=MESH)

    def c_copy(owner, to, sems):
        return pltpu.make_async_remote_copy(
            src_ref=cols.at[owner], dst_ref=cols.at[owner], send_sem=sems.at[owner], recv_sem=c_recv.at[owner],
            device_id={"blk": to}, device_id_type=MESH)

    @pl.when(b + 1 < nb)
    def _():
        c_copy(b, b + 1, c_right).start()

    @pl.when(b >= 1)
    def _():
        c_copy(b, b - 1, c_left).start()

    for off in range(1, ni):
        w_copy(i, lax.rem(i + off, ni)).start()

    r = res_ref[...]
    zero = jnp.zeros((n, 32), f32)
    gram_part = dot(r, jnp.concatenate([zero, zero, zero, r], axis=1), 0, 0)
    eye = lax.broadcasted_iota(jnp.int32, (n, n), 0) == lax.broadcasted_iota(jnp.int32, (n, n), 1)
    noise = jnp.sum(jnp.where(eye, noise_ref[...], 0.0), axis=1, keepdims=True)
    acc[...] = jnp.zeros_like(acc)

    def prepare(j):
        op, norms = row_operand(wrow[j])
        a_op[j] = op
        rn[j] = jnp.broadcast_to(norms, (n, 128))

    prepare(i)
    for off in range(1, ni):
        src = lax.rem(i - off + ni, ni)
        w_copy(src, src).wait_recv()
        prepare(src)

    reach = jnp.minimum(b, nb - 1 - b)

    @pl.loop(0, nb)
    def _(t):
        near = (t + 1) // 2
        paired = b + near * (1 - 2 * (t % 2))
        far = t - reach
        single = jnp.where(2 * b > nb - 1, b - far, b + far)
        owner = jnp.where(t <= 2 * reach, paired, single)

        @pl.when(t > 0)
        def _():
            c_copy(owner, b, c_right).wait_recv()

            @pl.when(jnp.logical_and(owner < b, b + 1 < nb))
            def _():
                c_copy(owner, b + 1, c_right).start()

            @pl.when(jnp.logical_and(owner > b, b >= 1))
            def _():
                c_copy(owner, b - 1, c_left).start()

        op, norms = col_operand(cols[owner, :h])
        b_op[...] = op
        cn[...] = norms
        d_op[...] = dir_operand(cols[owner, h:])

        @pl.loop(0, ni)
        def _(j):
            cross = dot(a_op[j], b_op[...], 1, 1, None)
            row_n = rn[j]
            x = cross + jnp.concatenate([row_n] * (n // 128), axis=1) + cn[0:1, :]
            x = jnp.maximum(x, 1e-30)
            v = x * lax.rsqrt(x)
            k = (1.0 + LN2 * v + (LN2 * LN2 / 3.0) * x) * jnp.exp2(-v)
            kh = k.astype(bf16)
            kl = (k - kh.astype(f32)).astype(bf16)
            acc[j] += dot(kh, d_op[...], 1, 0, None) + dot(kl, d_op[...], 1, 0, None)

    group = lanes((q, 128)) // 32

    def packed_part(j):
        a = acc[j]
        a = a + pltpu.roll(a, 32, 1)
        out = a[:q]
        for g in range(1, 4):
            out = jnp.where(group == g, a[g * q:(g + 1) * q], out)
        return out

    def p_copy(to, src):
        return pltpu.make_async_remote_copy(
            src_ref=parts.at[0, to], dst_ref=parts.at[1, src], send_sem=p_send.at[to], recv_sem=p_recv.at[src],
            device_id={"inner": to}, device_id_type=MESH)

    for off in range(1, ni):
        to = lax.rem(i + off, ni)
        parts[0, to] = packed_part(to)
        p_copy(to, i).start()
    image = packed_part(i)
    for off in range(1, ni):
        src = lax.rem(i - off + ni, ni)
        p_copy(src, src).wait_recv()
        image = image + parts[1, src]
    d = dir_ref[...]
    image = unpack4(image) + noise * d

    total = dot(image, jnp.concatenate([d, r, image, zero], axis=1), 0, 0) + gram_part

    def s_copy(buf, me, to, src, send, recv, axis):
        return pltpu.make_async_remote_copy(
            src_ref=buf.at[me], dst_ref=buf.at[src], send_sem=send.at[to], recv_sem=recv.at[src],
            device_id={axis: to}, device_id_type=MESH)

    sums_i[i] = total
    for off in range(1, ni):
        s_copy(sums_i, i, lax.rem(i + off, ni), i, si_send, si_recv, "inner").start()
    for off in range(1, ni):
        src = lax.rem(i - off + ni, ni)
        s_copy(sums_i, i, src, src, si_send, si_recv, "inner").wait_recv()
    total = sums_i[0]
    for j in range(1, ni):
        total = total + sums_i[j]
    sums_b[b] = total

    @pl.loop(1, nb)
    def _(off):
        s_copy(sums_b, b, lax.rem(b + off, nb), b, sb_send, sb_recv, "blk").start()

    @pl.loop(1, nb)
    def _(off):
        src = lax.rem(b - off + nb, nb)
        s_copy(sums_b, b, src, src, sb_send, sb_recv, "blk").wait_recv()

    total = lax.fori_loop(1, nb, lambda j, s: s + sums_b[j], sums_b[0])

    curv, qr, qq, gram = [total[:, 32 * g:32 * g + 32] for g in range(4)]
    curv = 0.5 * (curv + curv.T)
    unit = (lax.broadcasted_iota(jnp.int32, (32, 32), 0) == lax.broadcasted_iota(jnp.int32, (32, 32), 1)).astype(f32)
    alpha, gram_inv = eliminate([jnp.concatenate([curv, gram], axis=1), jnp.concatenate([gram, unit], axis=1)])
    change = qr - dot(qq, alpha, 1, 0)
    gram_next = gram - dot(qr, alpha, 0, 0) - dot(alpha, change, 0, 0)
    beta = dot(gram_inv, gram_next, 1, 0)
    r_next = r - dot(image, alpha, 1, 0)
    res_out[...] = r_next
    sol_out[...] = sol_ref[...] + dot(d, alpha, 1, 0)
    dir_out[...] = r_next + dot(d, beta, 1, 0)

    for off in range(1, ni):
        to = lax.rem(i + off, ni)
        w_copy(i, to).wait_send()
        p_copy(to, i).wait_send()
        s_copy(sums_i, i, to, i, si_send, si_recv, "inner").wait_send()

    @pl.loop(1, nb)
    def _(off):
        s_copy(sums_b, b, lax.rem(b + off, nb), b, sb_send, sb_recv, "blk").wait_send()

    @pl.loop(0, nb)
    def _(o):
        @pl.when(jnp.logical_and(o <= b, b + 1 < nb))
        def _():
            c_copy(o, b, c_right).wait_send()

        @pl.when(jnp.logical_and(o >= b, b >= 1))
        def _():
            c_copy(o, b, c_left).wait_send()


def solution(mesh):
    nb, ni = mesh.shape["blk"], mesh.shape["inner"]

    def shards(points, inverse_scale, noise_var, sol, residual, direction):
        n, feats = points.shape
        columns = direction.shape[1]
        dma = lambda k: pltpu.SemaphoreType.DMA((k,))
        vmem = pl.BlockSpec(memory_space=pltpu.VMEM)
        out = jax.ShapeDtypeStruct((n, columns), f32)
        return pl.pallas_call(
            functools.partial(kernel, nb, ni),
            out_shape=(out, out, out),
            in_specs=[vmem] * 6,
            out_specs=(vmem, vmem, vmem),
            scratch_shapes=[
                pltpu.VMEM((ni, n // 2, 128), f32),
                pltpu.VMEM((nb, n // 2 + n // 4, 128), f32),
                pltpu.VMEM((ni, n, 256), bf16),
                pltpu.VMEM((ni, n, 128), f32),
                pltpu.VMEM((n, 256), bf16),
                pltpu.VMEM((8, n), f32),
                pltpu.VMEM((n, 128), bf16),
                pltpu.VMEM((ni, n, 128), f32),
                pltpu.VMEM((2, ni, n // 4, 128), f32),
                pltpu.VMEM((ni, 32, 128), f32),
                pltpu.VMEM((nb, 32, 128), f32),
                dma(ni), dma(ni), dma(nb), dma(nb), dma(nb), dma(ni), dma(ni), dma(ni), dma(ni), dma(nb), dma(nb),
            ],
            compiler_params=pltpu.CompilerParams(
                collective_id=0, has_side_effects=True, vmem_limit_bytes=40 * 1024 * 1024),
        )(points, inverse_scale.reshape(1, feats), noise_var.reshape(1, n), sol, residual, direction)

    rows = P(("groups", "blk", "inner"), None)
    return jax.shard_map(
        shards, mesh=mesh,
        in_specs=(rows, P("groups"), P(("groups", "blk", "inner")), rows, rows, rows),
        out_specs=(rows, rows, rows), check_vma=False)
```

```python
import functools
import math

import jax
import jax.numpy as jnp
from jax import lax
from jax.experimental import pallas as pl
from jax.experimental.pallas import tpu as pltpu
from jax.sharding import PartitionSpec as P

MESH = pl.DeviceIdType.MESH
HIGH = lax.Precision.HIGHEST
LN2 = math.log(2.0)
FEATURE_SCALE = math.sqrt(5.0) / LN2
f32 = jnp.float32
bf16 = jnp.bfloat16


def dot(a, b, ca, cb, precision=HIGH):
    return lax.dot_general(a, b, (((ca,), (cb,)), ((), ())), precision=precision, preferred_element_type=f32)


def halves(x):
    hi = x.astype(bf16).astype(f32)
    lo = (x - hi).astype(bf16).astype(f32)
    return hi, lo


def row_operand(w):
    hi, lo = halves(w)
    both = jnp.concatenate([hi, lo], axis=0)
    norm = jnp.sum((hi + lo) * (hi + lo), axis=0, keepdims=True)
    both = (both.T * -2.0).astype(bf16)
    return jnp.concatenate([both, both], axis=1), jnp.broadcast_to(norm, (128, w.shape[1])).T


def col_operand(w):
    hi, lo = halves(w)
    norm = jnp.sum((hi + lo) * (hi + lo), axis=0, keepdims=True)
    hi, lo = hi.astype(bf16), lo.astype(bf16)
    return jnp.concatenate([hi, hi, lo, lo], axis=0), norm


def dir_operand(d):
    hi, lo = halves(d)
    return jnp.concatenate([hi, lo, jnp.zeros((64, d.shape[1]), f32)], axis=0).T.astype(bf16)


def eliminate(a):
    n = a.shape[0]
    rows = lax.broadcasted_iota(jnp.int32, (n, 1), 0)
    for k in range(n):
        pivot = a[k:k + 1, :] / a[k:k + 1, k:k + 1]
        column = jnp.where(rows == k, 0.0, a[:, k:k + 1])
        a = jnp.where(rows == k, pivot, a - column * pivot)
    return a[:, n:2 * n]


def kernel(nb, ni, points_hbm, scale_hbm, noise_hbm, sol_hbm, res_hbm, dir_hbm, sol_out, res_out, dir_out,
           pts, scale, noise, sol, res, wrow, cols, a_op, rn, b_op, cn, d_op, acc, parts,
           sums_i, sums_b, grams_i, grams_b, l_sem,
           w_send, w_recv, c_right, c_left, c_recv, p_send, p_recv, si_send, si_recv, sb_send, sb_recv,
           gi_send, gi_recv, gb_send, gb_recv):
    feats, n = pts.shape
    rhs = sol.shape[0]
    b = lax.axis_index("blk")
    i = lax.axis_index("inner")

    local = [
        pltpu.make_async_copy(points_hbm, pts, l_sem.at[0]),
        pltpu.make_async_copy(scale_hbm, scale, l_sem.at[1]),
        pltpu.make_async_copy(dir_hbm, cols.at[b, feats:], l_sem.at[2]),
        pltpu.make_async_copy(res_hbm, res, l_sem.at[3]),
        pltpu.make_async_copy(noise_hbm, noise, l_sem.at[4]),
        pltpu.make_async_copy(sol_hbm, sol, l_sem.at[5]),
    ]
    for copy in local:
        copy.start()

    barrier = pltpu.get_barrier_semaphore()
    for off in range(1, ni):
        pl.semaphore_signal(barrier, inc=1, device_id={"inner": lax.rem(i + off, ni)}, device_id_type=MESH)

    @pl.loop(1, nb)
    def _(off):
        pl.semaphore_signal(barrier, inc=1, device_id={"blk": lax.rem(b + off, nb)}, device_id_type=MESH)

    for copy in local:
        copy.wait()
    same = lax.broadcasted_iota(jnp.int32, (feats, feats), 0) == lax.broadcasted_iota(jnp.int32, (feats, feats), 1)
    factor = jnp.sum(jnp.where(same, scale[...] * FEATURE_SCALE, 0.0), axis=1, keepdims=True)
    own_w = pts[...] * factor
    cols[b, :feats] = own_w
    pl.semaphore_wait(barrier, ni + nb - 2)

    def w_copy(to, src):
        return pltpu.make_async_remote_copy(
            src_ref=cols.at[b, :feats], dst_ref=wrow.at[src], send_sem=w_send.at[to], recv_sem=w_recv.at[src],
            device_id={"inner": to}, device_id_type=MESH)

    def c_copy(owner, to, sems):
        return pltpu.make_async_remote_copy(
            src_ref=cols.at[owner], dst_ref=cols.at[owner], send_sem=sems.at[owner], recv_sem=c_recv.at[owner],
            device_id={"blk": to}, device_id_type=MESH)

    @pl.when(b + 1 < nb)
    def _():
        c_copy(b, b + 1, c_right).start()

    @pl.when(b >= 1)
    def _():
        c_copy(b, b - 1, c_left).start()

    for off in range(1, ni):
        w_copy(lax.rem(i + off, ni), i).start()

    def s_copy(buf, me, to, src, send, recv, axis):
        return pltpu.make_async_remote_copy(
            src_ref=buf.at[me], dst_ref=buf.at[src], send_sem=send.at[to], recv_sem=recv.at[src],
            device_id={axis: to}, device_id_type=MESH)

    def inner_send(buf, send, recv):
        for off in range(1, ni):
            s_copy(buf, i, lax.rem(i + off, ni), i, send, recv, "inner").start()

    def inner_sum(buf, send, recv):
        for off in range(1, ni):
            src = lax.rem(i - off + ni, ni)
            s_copy(buf, i, src, src, send, recv, "inner").wait_recv()
        total = buf[0]
        for j in range(1, ni):
            total = total + buf[j]
        return total

    def blk_send(buf, send, recv):
        @pl.loop(1, nb)
        def _(off):
            s_copy(buf, b, lax.rem(b + off, nb), b, send, recv, "blk").start()

    def blk_sum(buf, send, recv):
        @pl.loop(1, nb)
        def _(off):
            src = lax.rem(b - off + nb, nb)
            s_copy(buf, b, src, src, send, recv, "blk").wait_recv()
        return lax.fori_loop(1, nb, lambda j, s: s + buf[j], buf[0])

    r = res[...]
    grams_i[i] = dot(r, r, 1, 1)
    inner_send(grams_i, gi_send, gi_recv)
    acc[...] = jnp.zeros_like(acc)

    def prepare(j, w):
        op, norms = row_operand(w)
        a_op[j] = op
        rn[j] = norms

    def load_column(owner):
        op, norms = col_operand(cols[owner, :feats])
        b_op[...] = op
        cn[...] = norms
        d_op[...] = dir_operand(cols[owner, feats:])

    def tile(j):
        cross = dot(a_op[j], b_op[...], 1, 0, None)
        row_n = rn[j]
        x = cross + jnp.concatenate([row_n] * (n // 128), axis=1) + cn[...]
        x = jnp.maximum(x, 1e-30)
        v = x * lax.rsqrt(x)
        k = (1.0 + LN2 * v + (LN2 * LN2 / 3.0) * x) * jnp.exp2(-v)
        kh = k.astype(bf16)
        kl = (k - kh.astype(f32)).astype(bf16)
        return acc[j] + dot(kh, d_op[...], 1, 0, None) + dot(kl, d_op[...], 1, 0, None)

    prepare(i, own_w)
    load_column(b)

    @pl.loop(0, ni)
    def _(off):
        j = lax.rem(i - off + ni, ni)

        @pl.when(off > 0)
        def _():
            w_copy(j, j).wait_recv()
            prepare(j, wrow[j])

        acc[j] = tile(j)

    grams_b[b] = inner_sum(grams_i, gi_send, gi_recv)
    blk_send(grams_b, gb_send, gb_recv)

    reach = jnp.minimum(b, nb - 1 - b)

    def receive(t):
        near = (t + 1) // 2
        paired = b + near * (1 - 2 * (t % 2))
        far = t - reach
        single = jnp.where(2 * b > nb - 1, b - far, b + far)
        owner = jnp.where(t <= 2 * reach, paired, single)
        c_copy(owner, b, c_right).wait_recv()

        @pl.when(jnp.logical_and(owner < b, b + 1 < nb))
        def _():
            c_copy(owner, b + 1, c_right).start()

        @pl.when(jnp.logical_and(owner > b, b >= 1))
        def _():
            c_copy(owner, b - 1, c_left).start()

        load_column(owner)

    @pl.loop(1, nb - 1)
    def _(t):
        receive(t)

        @pl.loop(0, ni)
        def _(j):
            acc[j] = tile(j)

    gram = blk_sum(grams_b, gb_send, gb_recv)
    unit = (lax.broadcasted_iota(jnp.int32, (rhs, rhs), 0) == lax.broadcasted_iota(jnp.int32, (rhs, rhs), 1)).astype(f32)
    gram_inv = eliminate(jnp.concatenate([gram, unit], axis=1))

    receive(nb - 1)

    def p_copy(to, src):
        return pltpu.make_async_remote_copy(
            src_ref=parts.at[0, to], dst_ref=parts.at[1, src], send_sem=p_send.at[to], recv_sem=p_recv.at[src],
            device_id={"inner": to}, device_id_type=MESH)

    def finished(j):
        a = tile(j).T
        return a[:rhs] + a[rhs:2 * rhs]

    @pl.loop(1, ni)
    def _(off):
        to = lax.rem(i + off, ni)
        parts[0, to] = finished(to)
        p_copy(to, i).start()

    d = cols[b, feats:]
    image = finished(i) + noise[...] * d
    for off in range(1, ni):
        src = lax.rem(i - off + ni, ni)
        p_copy(src, src).wait_recv()
        image = image + parts[1, src]

    sums_i[i] = dot(image, jnp.concatenate([d, r, image], axis=0), 1, 1)
    inner_send(sums_i, si_send, si_recv)
    sums_b[b] = inner_sum(sums_i, si_send, si_recv)
    blk_send(sums_b, sb_send, sb_recv)
    total = blk_sum(sums_b, sb_send, sb_recv)

    curv, qr, qq = [total[:, rhs * g:rhs * (g + 1)] for g in range(3)]
    curv = 0.5 * (curv + curv.T)
    alpha = eliminate(jnp.concatenate([curv, gram], axis=1))
    alpha_t = alpha.T
    r_next = r - dot(alpha_t, image, 1, 0)
    change = qr - dot(qq, alpha, 1, 0)
    gram_next = gram - dot(alpha_t, qr, 1, 0).T - dot(alpha_t, change, 1, 0)
    beta = dot(gram_inv, gram_next, 1, 0)
    res_out[...] = r_next
    sol_out[...] = sol[...] + dot(alpha_t, d, 1, 0)
    dir_out[...] = r_next + dot(beta.T, d, 1, 0)

    for off in range(1, ni):
        to = lax.rem(i + off, ni)
        w_copy(to, i).wait_send()
        p_copy(to, i).wait_send()
        s_copy(sums_i, i, to, i, si_send, si_recv, "inner").wait_send()
        s_copy(grams_i, i, to, i, gi_send, gi_recv, "inner").wait_send()

    @pl.loop(1, nb)
    def _(off):
        to = lax.rem(b + off, nb)
        s_copy(sums_b, b, to, b, sb_send, sb_recv, "blk").wait_send()
        s_copy(grams_b, b, to, b, gb_send, gb_recv, "blk").wait_send()

    @pl.loop(0, nb)
    def _(o):
        @pl.when(jnp.logical_and(o <= b, b + 1 < nb))
        def _():
            c_copy(o, b, c_right).wait_send()

        @pl.when(jnp.logical_and(o >= b, b >= 1))
        def _():
            c_copy(o, b, c_left).wait_send()


def solution(mesh):
    nb, ni = mesh.shape["blk"], mesh.shape["inner"]

    def shards(points, inverse_scale, noise_var, sol, residual, direction):
        n, feats = points.shape
        rhs = direction.shape[1]
        dma = lambda k: pltpu.SemaphoreType.DMA((k,))
        vmem = pl.BlockSpec(memory_space=pltpu.VMEM)
        out = jax.ShapeDtypeStruct((rhs, n), f32)
        results = pl.pallas_call(
            functools.partial(kernel, nb, ni),
            out_shape=(out, out, out),
            in_specs=[pl.BlockSpec(memory_space=pl.ANY)] * 6,
            out_specs=(vmem, vmem, vmem),
            scratch_shapes=[
                pltpu.VMEM((feats, n), f32),
                pltpu.VMEM((1, feats), f32),
                pltpu.VMEM((1, n), f32),
                pltpu.VMEM((rhs, n), f32),
                pltpu.VMEM((rhs, n), f32),
                pltpu.VMEM((ni, feats, n), f32),
                pltpu.VMEM((nb, feats + rhs, n), f32),
                pltpu.VMEM((ni, n, 4 * feats), bf16),
                pltpu.VMEM((ni, n, 128), f32),
                pltpu.VMEM((4 * feats, n), bf16),
                pltpu.VMEM((1, n), f32),
                pltpu.VMEM((n, 128), bf16),
                pltpu.VMEM((ni, n, 128), f32),
                pltpu.VMEM((2, ni, rhs, n), f32),
                pltpu.VMEM((ni, rhs, 3 * rhs), f32),
                pltpu.VMEM((nb, rhs, 3 * rhs), f32),
                pltpu.VMEM((ni, rhs, rhs), f32),
                pltpu.VMEM((nb, rhs, rhs), f32),
                dma(6),
                dma(ni), dma(ni), dma(nb), dma(nb), dma(nb), dma(ni), dma(ni), dma(ni), dma(ni), dma(nb), dma(nb),
                dma(ni), dma(ni), dma(nb), dma(nb),
            ],
            compiler_params=pltpu.CompilerParams(
                collective_id=0, has_side_effects=True, vmem_limit_bytes=60 * 1024 * 1024),
        )(points.T, inverse_scale.reshape(1, feats), noise_var.reshape(1, n), sol.T, residual.T, direction.T)
        return tuple(x.T for x in results)

    rows = P(("groups", "blk", "inner"), None)
    return jax.shard_map(
        shards, mesh=mesh,
        in_specs=(rows, P("groups"), P(("groups", "blk", "inner")), rows, rows, rows),
        out_specs=(rows, rows, rows), check_vma=False)
```

```python
import functools
import math

import jax
import jax.numpy as jnp
from jax import lax
from jax.experimental import pallas as pl
from jax.experimental.pallas import tpu as pltpu
from jax.sharding import PartitionSpec as P

MESH = pl.DeviceIdType.MESH
HIGH = lax.Precision.HIGHEST
LN2 = math.log(2.0)
FEATURE_SCALE = math.sqrt(5.0) / LN2
f32 = jnp.float32
bf16 = jnp.bfloat16


def dot(a, b, ca, cb, precision=HIGH):
    return lax.dot_general(a, b, (((ca,), (cb,)), ((), ())), precision=precision, preferred_element_type=f32)


def halves(x):
    hi = x.astype(bf16).astype(f32)
    lo = (x - hi).astype(bf16).astype(f32)
    return hi, lo


def row_operand(w):
    hi, lo = halves(w)
    both = jnp.concatenate([hi, lo], axis=0)
    norm = jnp.sum((hi + lo) * (hi + lo), axis=0, keepdims=True)
    both = (both.T * -2.0).astype(bf16)
    return jnp.concatenate([both, both], axis=1), jnp.broadcast_to(norm, (128, w.shape[1])).T


def col_operand(w):
    hi, lo = halves(w)
    norm = jnp.sum((hi + lo) * (hi + lo), axis=0, keepdims=True)
    hi, lo = hi.astype(bf16), lo.astype(bf16)
    return jnp.concatenate([hi, hi, lo, lo], axis=0), norm


def dir_operand(d):
    hi, lo = halves(d)
    return jnp.concatenate([hi, lo, jnp.zeros((64, d.shape[1]), f32)], axis=0).T.astype(bf16)


def eliminate(a, first, last):
    rows = lax.broadcasted_iota(jnp.int32, (a.shape[0], 1), 0)
    for k in range(first, last, 2):
        r0, r1 = a[k:k + 1, :], a[k + 1:k + 2, :]
        c0, c1 = a[:, k:k + 1], a[:, k + 1:k + 2]
        p01 = a[k:k + 1, k + 1:k + 2]
        inv0 = 1.0 / a[k:k + 1, k:k + 1]
        low = a[k + 1:k + 2, k:k + 1] * inv0
        inv1 = 1.0 / (a[k + 1:k + 2, k + 1:k + 2] - low * p01)
        r1 = (r1 - low * r0) * inv1
        r0 = (r0 - p01 * r1) * inv0
        a = jnp.where(rows == k, r0, jnp.where(rows == k + 1, r1, a - c0 * r0 - c1 * r1))
    return a


def pack4(x):
    n = x.shape[0] // 4
    return jnp.concatenate([x[g * n:(g + 1) * n] for g in range(4)], axis=1)


def unpack4(x):
    n = x.shape[1] // 4
    return jnp.concatenate([x[:, g * n:(g + 1) * n] for g in range(4)], axis=0)


def kernel(nb, ni, points_hbm, scale_hbm, noise_hbm, sol_hbm, res_hbm, dir_hbm, sol_out, res_out, dir_out,
           pts, scale, noise, sol, res, wrow, cols, a_op, rn, b_op, cn, d_op, acc, parts,
           sums_i, sums_b, grams_i, grams_b, curv_i, curv_b, l_sem,
           w_send, w_recv, c_right, c_left, c_recv, p_send, p_recv, si_send, si_recv, sb_send, sb_recv,
           gi_send, gi_recv, gb_send, gb_recv, ci_send, ci_recv, cb_send, cb_recv):
    feats, n = pts.shape
    rhs = sol.shape[0]
    b = lax.axis_index("blk")
    i = lax.axis_index("inner")

    local = [
        pltpu.make_async_copy(points_hbm, pts, l_sem.at[0]),
        pltpu.make_async_copy(scale_hbm, scale, l_sem.at[1]),
        pltpu.make_async_copy(dir_hbm, cols.at[b, feats:], l_sem.at[2]),
        pltpu.make_async_copy(res_hbm, res, l_sem.at[3]),
        pltpu.make_async_copy(noise_hbm, noise, l_sem.at[4]),
        pltpu.make_async_copy(sol_hbm, sol, l_sem.at[5]),
    ]
    for copy in local:
        copy.start()

    barrier = pltpu.get_barrier_semaphore()
    for off in range(1, ni):
        pl.semaphore_signal(barrier, inc=1, device_id={"inner": lax.rem(i + off, ni)}, device_id_type=MESH)

    @pl.loop(1, nb)
    def _(off):
        pl.semaphore_signal(barrier, inc=1, device_id={"blk": lax.rem(b + off, nb)}, device_id_type=MESH)

    for copy in local:
        copy.wait()
    same = lax.broadcasted_iota(jnp.int32, (feats, feats), 0) == lax.broadcasted_iota(jnp.int32, (feats, feats), 1)
    factor = jnp.sum(jnp.where(same, scale[...] * FEATURE_SCALE, 0.0), axis=1, keepdims=True)
    own_w = pts[...] * factor
    cols[b, :feats] = own_w
    pl.semaphore_wait(barrier, ni + nb - 2)

    def w_copy(to, src):
        return pltpu.make_async_remote_copy(
            src_ref=cols.at[b, :feats], dst_ref=wrow.at[src], send_sem=w_send.at[to], recv_sem=w_recv.at[src],
            device_id={"inner": to}, device_id_type=MESH)

    def c_copy(owner, to, sems):
        return pltpu.make_async_remote_copy(
            src_ref=cols.at[owner], dst_ref=cols.at[owner], send_sem=sems.at[owner], recv_sem=c_recv.at[owner],
            device_id={"blk": to}, device_id_type=MESH)

    @pl.when(b + 1 < nb)
    def _():
        c_copy(b, b + 1, c_right).start()

    @pl.when(b >= 1)
    def _():
        c_copy(b, b - 1, c_left).start()

    for off in range(1, ni):
        w_copy(lax.rem(i + off, ni), i).start()

    def s_copy(buf, me, to, src, send, recv, axis):
        return pltpu.make_async_remote_copy(
            src_ref=buf.at[me], dst_ref=buf.at[src], send_sem=send.at[to], recv_sem=recv.at[src],
            device_id={axis: to}, device_id_type=MESH)

    def inner_send(buf, send, recv):
        for off in range(1, ni):
            s_copy(buf, i, lax.rem(i + off, ni), i, send, recv, "inner").start()

    def inner_sum(buf, send, recv):
        for off in range(1, ni):
            src = lax.rem(i - off + ni, ni)
            s_copy(buf, i, src, src, send, recv, "inner").wait_recv()
        total = buf[0]
        for j in range(1, ni):
            total = total + buf[j]
        return total

    def blk_send(buf, send, recv):
        @pl.loop(1, nb)
        def _(off):
            s_copy(buf, b, lax.rem(b + off, nb), b, send, recv, "blk").start()

    def blk_sum(buf, send, recv):
        @pl.loop(1, nb)
        def _(off):
            src = lax.rem(b - off + nb, nb)
            s_copy(buf, b, src, src, send, recv, "blk").wait_recv()
        return lax.fori_loop(1, nb, lambda j, s: s + buf[j], buf[0])

    r = res[...]
    grams_i[i] = pack4(dot(r, r, 1, 1))
    inner_send(grams_i, gi_send, gi_recv)
    acc[...] = jnp.zeros_like(acc)

    def prepare(j, w):
        op, norms = row_operand(w)
        a_op[j] = op
        rn[j] = norms

    def load_column(owner):
        op, norms = col_operand(cols[owner, :feats])
        b_op[...] = op
        cn[...] = norms
        d_op[...] = dir_operand(cols[owner, feats:])

    def tile(j):
        cross = dot(a_op[j], b_op[...], 1, 0, None)
        row_n = rn[j]
        x = cross + jnp.concatenate([row_n] * (n // 128), axis=1) + cn[...]
        x = jnp.maximum(x, 1e-30)
        v = x * lax.rsqrt(x)
        k = (1.0 + LN2 * v + (LN2 * LN2 / 3.0) * x) * jnp.exp2(-v)
        kh = k.astype(bf16)
        kl = (k - kh.astype(f32)).astype(bf16)
        return acc[j] + dot(kh, d_op[...], 1, 0, None) + dot(kl, d_op[...], 1, 0, None)

    prepare(i, own_w)
    load_column(b)

    @pl.loop(0, ni)
    def _(off):
        j = lax.rem(i - off + ni, ni)

        @pl.when(off > 0)
        def _():
            w_copy(j, j).wait_recv()
            prepare(j, wrow[j])

        acc[j] = tile(j)

    grams_b[b] = inner_sum(grams_i, gi_send, gi_recv)
    blk_send(grams_b, gb_send, gb_recv)

    reach = jnp.minimum(b, nb - 1 - b)

    def receive(t):
        near = (t + 1) // 2
        paired = b + near * (1 - 2 * (t % 2))
        far = t - reach
        single = jnp.where(2 * b > nb - 1, b - far, b + far)
        owner = jnp.where(t <= 2 * reach, paired, single)
        c_copy(owner, b, c_right).wait_recv()

        @pl.when(jnp.logical_and(owner < b, b + 1 < nb))
        def _():
            c_copy(owner, b + 1, c_right).start()

        @pl.when(jnp.logical_and(owner > b, b >= 1))
        def _():
            c_copy(owner, b - 1, c_left).start()

        load_column(owner)

    @pl.loop(1, nb - 1)
    def _(t):
        receive(t)

        @pl.loop(0, ni)
        def _(j):
            acc[j] = tile(j)


    receive(nb - 1)

    def p_copy(to, src):
        return pltpu.make_async_remote_copy(
            src_ref=parts.at[0, to], dst_ref=parts.at[1, src], send_sem=p_send.at[to], recv_sem=p_recv.at[src],
            device_id={"inner": to}, device_id_type=MESH)

    def finished(j):
        a = tile(j).T
        return a[:rhs] + a[rhs:2 * rhs]

    @pl.loop(1, ni)
    def _(off):
        to = lax.rem(i + off, ni)
        parts[0, to] = finished(to)
        p_copy(to, i).start()

    d = cols[b, feats:]
    image = finished(i) + noise[...] * d
    for off in range(1, ni):
        src = lax.rem(i - off + ni, ni)
        p_copy(src, src).wait_recv()
        image = image + parts[1, src]

    curv_i[i] = pack4(dot(d, image, 1, 1))
    inner_send(curv_i, ci_send, ci_recv)
    rest = dot(jnp.concatenate([r, image], axis=0), image, 1, 1)
    sums_i[i] = pack4(rest)
    inner_send(sums_i, si_send, si_recv)
    gram = unpack4(blk_sum(grams_b, gb_send, gb_recv))
    unit = (lax.broadcasted_iota(jnp.int32, (rhs, rhs), 0) == lax.broadcasted_iota(jnp.int32, (rhs, rhs), 1)).astype(f32)
    inverse = eliminate(jnp.concatenate([gram, unit], axis=1), 0, rhs // 2)
    curv_b[b] = inner_sum(curv_i, ci_send, ci_recv)
    blk_send(curv_b, cb_send, cb_recv)
    sums_b[b] = inner_sum(sums_i, si_send, si_recv)
    blk_send(sums_b, sb_send, sb_recv)
    gram_inv = eliminate(inverse, rhs // 2, rhs)[:, rhs:]
    curv = unpack4(blk_sum(curv_b, cb_send, cb_recv))
    curv = 0.5 * (curv + curv.T)
    alpha = eliminate(jnp.concatenate([curv, gram], axis=1), 0, rhs)[:, rhs:]
    rest = unpack4(blk_sum(sums_b, sb_send, sb_recv))
    rq, qq = rest[:rhs], rest[rhs:]
    alpha_t = alpha.T
    r_next = r - dot(alpha_t, image, 1, 0)
    change = rq.T - dot(qq, alpha, 1, 0)
    gram_next = gram - dot(rq, alpha, 1, 0) - dot(alpha_t, change, 1, 0)
    beta = dot(gram_inv, gram_next, 1, 0)
    res_out[...] = r_next
    sol_out[...] = sol[...] + dot(alpha_t, d, 1, 0)
    dir_out[...] = r_next + dot(beta.T, d, 1, 0)

    for off in range(1, ni):
        to = lax.rem(i + off, ni)
        w_copy(to, i).wait_send()
        p_copy(to, i).wait_send()
        s_copy(sums_i, i, to, i, si_send, si_recv, "inner").wait_send()
        s_copy(grams_i, i, to, i, gi_send, gi_recv, "inner").wait_send()
        s_copy(curv_i, i, to, i, ci_send, ci_recv, "inner").wait_send()

    @pl.loop(1, nb)
    def _(off):
        to = lax.rem(b + off, nb)
        s_copy(sums_b, b, to, b, sb_send, sb_recv, "blk").wait_send()
        s_copy(grams_b, b, to, b, gb_send, gb_recv, "blk").wait_send()
        s_copy(curv_b, b, to, b, cb_send, cb_recv, "blk").wait_send()

    @pl.loop(0, nb)
    def _(o):
        @pl.when(jnp.logical_and(o <= b, b + 1 < nb))
        def _():
            c_copy(o, b, c_right).wait_send()

        @pl.when(jnp.logical_and(o >= b, b >= 1))
        def _():
            c_copy(o, b, c_left).wait_send()


def write_out(a, b, c, a_out, b_out, c_out, sems):
    copies = [pltpu.make_async_copy(x, y, sems.at[k]) for k, (x, y) in enumerate(((a, a_out), (b, b_out), (c, c_out)))]
    for copy in copies:
        copy.start()
    for copy in copies:
        copy.wait()


def solution(mesh):
    nb, ni = mesh.shape["blk"], mesh.shape["inner"]

    def shards(points, inverse_scale, noise_var, sol, residual, direction):
        n, feats = points.shape
        rhs = direction.shape[1]
        dma = lambda k: pltpu.SemaphoreType.DMA((k,))
        vmem = pl.BlockSpec(memory_space=pltpu.VMEM)
        out = jax.ShapeDtypeStruct((rhs, n), f32)
        results = pl.pallas_call(
            functools.partial(kernel, nb, ni),
            out_shape=(out, out, out),
            in_specs=[pl.BlockSpec(memory_space=pltpu.HBM)] * 6,
            out_specs=(vmem, vmem, vmem),
            scratch_shapes=[
                pltpu.VMEM((feats, n), f32),
                pltpu.VMEM((1, feats), f32),
                pltpu.VMEM((1, n), f32),
                pltpu.VMEM((rhs, n), f32),
                pltpu.VMEM((rhs, n), f32),
                pltpu.VMEM((ni, feats, n), f32),
                pltpu.VMEM((nb, feats + rhs, n), f32),
                pltpu.VMEM((ni, n, 4 * feats), bf16),
                pltpu.VMEM((ni, n, 128), f32),
                pltpu.VMEM((4 * feats, n), bf16),
                pltpu.VMEM((1, n), f32),
                pltpu.VMEM((n, 128), bf16),
                pltpu.VMEM((ni, n, 128), f32),
                pltpu.VMEM((2, ni, rhs, n), f32),
                pltpu.VMEM((ni, rhs // 2, 4 * rhs), f32),
                pltpu.VMEM((nb, rhs // 2, 4 * rhs), f32),
                pltpu.VMEM((ni, rhs // 4, 4 * rhs), f32),
                pltpu.VMEM((nb, rhs // 4, 4 * rhs), f32),
                pltpu.VMEM((ni, rhs // 4, 4 * rhs), f32),
                pltpu.VMEM((nb, rhs // 4, 4 * rhs), f32),
                dma(6),
                dma(ni), dma(ni), dma(nb), dma(nb), dma(nb), dma(ni), dma(ni), dma(ni), dma(ni), dma(nb), dma(nb),
                dma(ni), dma(ni), dma(nb), dma(nb), dma(ni), dma(ni), dma(nb), dma(nb),
            ],
            compiler_params=pltpu.CompilerParams(
                collective_id=0, has_side_effects=True, vmem_limit_bytes=60 * 1024 * 1024),
        )(points.T, inverse_scale.reshape(1, feats), noise_var.reshape(1, n), sol.T, residual.T, direction.T)
        results = pl.pallas_call(
            write_out, out_shape=(out, out, out), in_specs=[vmem] * 3,
            out_specs=[pl.BlockSpec(memory_space=pltpu.HBM)] * 3, scratch_shapes=[dma(3)])(*results)
        return tuple(x.T for x in results)

    rows = P(("groups", "blk", "inner"), None)
    return jax.shard_map(
        shards, mesh=mesh,
        in_specs=(rows, P("groups"), P(("groups", "blk", "inner")), rows, rows, rows),
        out_specs=(rows, rows, rows), check_vma=False)
```

```python
import functools
import math

import jax
import jax.numpy as jnp
from jax import lax
from jax.experimental import pallas as pl
from jax.experimental.pallas import tpu as pltpu
from jax.sharding import PartitionSpec as P

MESH = pl.DeviceIdType.MESH
HIGH = lax.Precision.HIGHEST
LN2 = math.log(2.0)
FEATURE_SCALE = math.sqrt(5.0) / LN2
f32 = jnp.float32
bf16 = jnp.bfloat16


def dot(a, b, ca, cb, precision=HIGH):
    return lax.dot_general(a, b, (((ca,), (cb,)), ((), ())), precision=precision, preferred_element_type=f32)


def halves(x):
    hi = x.astype(bf16).astype(f32)
    lo = (x - hi).astype(bf16).astype(f32)
    return hi, lo


def row_operand(w):
    hi, lo = halves(w)
    both = jnp.concatenate([hi, lo], axis=0)
    norm = jnp.sum((hi + lo) * (hi + lo), axis=0, keepdims=True)
    both = (both.T * -2.0).astype(bf16)
    return jnp.concatenate([both, both], axis=1), jnp.broadcast_to(norm, (128, w.shape[1])).T


def col_operand(w):
    hi, lo = halves(w)
    norm = jnp.sum((hi + lo) * (hi + lo), axis=0, keepdims=True)
    hi, lo = hi.astype(bf16), lo.astype(bf16)
    return jnp.concatenate([hi, hi, lo, lo], axis=0), norm


def dir_operand(d):
    hi, lo = halves(d)
    return jnp.concatenate([hi, lo, jnp.zeros((64, d.shape[1]), f32)], axis=0).T.astype(bf16)


def eliminate(a, first, last):
    rows = lax.broadcasted_iota(jnp.int32, (a.shape[0], 1), 0)
    for k in range(first, last, 2):
        r0, r1 = a[k:k + 1, :], a[k + 1:k + 2, :]
        c0, c1 = a[:, k:k + 1], a[:, k + 1:k + 2]
        p01 = a[k:k + 1, k + 1:k + 2]
        inv0 = 1.0 / a[k:k + 1, k:k + 1]
        low = a[k + 1:k + 2, k:k + 1] * inv0
        inv1 = 1.0 / (a[k + 1:k + 2, k + 1:k + 2] - low * p01)
        r1 = (r1 - low * r0) * inv1
        r0 = (r0 - p01 * r1) * inv0
        a = jnp.where(rows == k, r0, jnp.where(rows == k + 1, r1, a - c0 * r0 - c1 * r1))
    return a


def pack4(x):
    n = x.shape[0] // 4
    return jnp.concatenate([x[g * n:(g + 1) * n] for g in range(4)], axis=1)


def unpack4(x):
    n = x.shape[1] // 4
    return jnp.concatenate([x[:, g * n:(g + 1) * n] for g in range(4)], axis=0)


def kernel(nb, ni, points_hbm, scale_hbm, noise_hbm, sol_hbm, res_hbm, dir_hbm, sol_out, res_out, dir_out,
           pts, scale, noise, sol, res, wrow, cols, a_op, rn, b_op, cn, d_op, acc, parts,
           sums_i, sums_b, grams_i, grams_b, curv_i, curv_b, l_sem,
           w_send, w_recv, c_send, c_recv, p_send, p_recv, si_send, si_recv, sb_send, sb_recv,
           gi_send, gi_recv, gb_send, gb_recv, ci_send, ci_recv, cb_send, cb_recv):
    feats, n = pts.shape
    rhs = sol.shape[0]
    b = lax.axis_index("blk")
    i = lax.axis_index("inner")

    local = [
        pltpu.make_async_copy(points_hbm, pts, l_sem.at[0]),
        pltpu.make_async_copy(scale_hbm, scale, l_sem.at[1]),
        pltpu.make_async_copy(dir_hbm, cols.at[b, feats:], l_sem.at[2]),
        pltpu.make_async_copy(res_hbm, res, l_sem.at[3]),
        pltpu.make_async_copy(noise_hbm, noise, l_sem.at[4]),
        pltpu.make_async_copy(sol_hbm, sol, l_sem.at[5]),
    ]
    for copy in local:
        copy.start()

    barrier = pltpu.get_barrier_semaphore()
    for off in range(1, ni):
        pl.semaphore_signal(barrier, inc=1, device_id={"inner": lax.rem(i + off, ni)}, device_id_type=MESH)

    @pl.loop(1, nb)
    def _(off):
        pl.semaphore_signal(barrier, inc=1, device_id={"blk": lax.rem(b + off, nb)}, device_id_type=MESH)

    for copy in local:
        copy.wait()
    same = lax.broadcasted_iota(jnp.int32, (feats, feats), 0) == lax.broadcasted_iota(jnp.int32, (feats, feats), 1)
    factor = jnp.sum(jnp.where(same, scale[...] * FEATURE_SCALE, 0.0), axis=1, keepdims=True)
    own_w = pts[...] * factor
    cols[b, :feats] = own_w
    pl.semaphore_wait(barrier, ni + nb - 2)

    def w_copy(to, src):
        return pltpu.make_async_remote_copy(
            src_ref=cols.at[b, :feats], dst_ref=wrow.at[src], send_sem=w_send.at[to], recv_sem=w_recv.at[src],
            device_id={"inner": to}, device_id_type=MESH)

    def c_copy(to, owner):
        return pltpu.make_async_remote_copy(
            src_ref=cols.at[owner], dst_ref=cols.at[owner], send_sem=c_send.at[to], recv_sem=c_recv.at[owner],
            device_id={"blk": to}, device_id_type=MESH)

    reach = jnp.minimum(b, nb - 1 - b)

    def owner_at(t):
        near = (t + 1) // 2
        paired = b + near * (1 - 2 * (t % 2))
        far = t - reach
        single = jnp.where(2 * b > nb - 1, b - far, b + far)
        return jnp.where(t <= 2 * reach, paired, single)

    @pl.loop(1, nb)
    def _(t):
        c_copy(owner_at(t), b).start()

    for off in range(1, ni):
        w_copy(lax.rem(i + off, ni), i).start()

    def s_copy(buf, me, to, src, send, recv, axis):
        return pltpu.make_async_remote_copy(
            src_ref=buf.at[me], dst_ref=buf.at[src], send_sem=send.at[to], recv_sem=recv.at[src],
            device_id={axis: to}, device_id_type=MESH)

    def inner_send(buf, send, recv):
        for off in range(1, ni):
            s_copy(buf, i, lax.rem(i + off, ni), i, send, recv, "inner").start()

    def inner_sum(buf, send, recv):
        for off in range(1, ni):
            src = lax.rem(i - off + ni, ni)
            s_copy(buf, i, src, src, send, recv, "inner").wait_recv()
        total = buf[0]
        for j in range(1, ni):
            total = total + buf[j]
        return total

    def blk_send(buf, send, recv):
        @pl.loop(1, nb)
        def _(off):
            s_copy(buf, b, lax.rem(b + off, nb), b, send, recv, "blk").start()

    def blk_sum(buf, send, recv):
        @pl.loop(1, nb)
        def _(off):
            src = lax.rem(b - off + nb, nb)
            s_copy(buf, b, src, src, send, recv, "blk").wait_recv()
        return lax.fori_loop(1, nb, lambda j, s: s + buf[j], buf[0])

    r = res[...]
    grams_i[i] = pack4(dot(r, r, 1, 1))
    inner_send(grams_i, gi_send, gi_recv)
    acc[...] = jnp.zeros_like(acc)

    def prepare(j, w):
        op, norms = row_operand(w)
        a_op[j] = op
        rn[j] = norms

    def load_column(owner):
        op, norms = col_operand(cols[owner, :feats])
        b_op[...] = op
        cn[...] = norms
        d_op[...] = dir_operand(cols[owner, feats:])

    def tile(j):
        cross = dot(a_op[j], b_op[...], 1, 0, None)
        row_n = rn[j]
        x = cross + jnp.concatenate([row_n] * (n // 128), axis=1) + cn[...]
        x = jnp.maximum(x, 1e-30)
        v = x * lax.rsqrt(x)
        k = (1.0 + LN2 * v + (LN2 * LN2 / 3.0) * x) * jnp.exp2(-v)
        kh = k.astype(bf16)
        kl = (k - kh.astype(f32)).astype(bf16)
        return acc[j] + dot(kh, d_op[...], 1, 0, None) + dot(kl, d_op[...], 1, 0, None)

    prepare(i, own_w)
    load_column(b)

    @pl.loop(0, ni)
    def _(off):
        j = lax.rem(i - off + ni, ni)

        @pl.when(off > 0)
        def _():
            w_copy(j, j).wait_recv()
            prepare(j, wrow[j])

        acc[j] = tile(j)

    grams_b[b] = inner_sum(grams_i, gi_send, gi_recv)
    blk_send(grams_b, gb_send, gb_recv)

    def receive(t):
        owner = owner_at(t)
        c_copy(owner, owner).wait_recv()
        load_column(owner)

    @pl.loop(1, nb - 1)
    def _(t):
        receive(t)

        @pl.loop(0, ni, unroll=ni)
        def _(j):
            acc[j] = tile(j)


    receive(nb - 1)

    def p_copy(to, src):
        return pltpu.make_async_remote_copy(
            src_ref=parts.at[0, to], dst_ref=parts.at[1, src], send_sem=p_send.at[to], recv_sem=p_recv.at[src],
            device_id={"inner": to}, device_id_type=MESH)

    def finished(j):
        a = tile(j).T
        return a[:rhs] + a[rhs:2 * rhs]

    @pl.loop(1, ni, unroll=ni - 1)
    def _(off):
        to = lax.rem(i + off, ni)
        parts[0, to] = finished(to)
        p_copy(to, i).start()

    d = cols[b, feats:]
    image = finished(i) + noise[...] * d
    for off in range(1, ni):
        src = lax.rem(i - off + ni, ni)
        p_copy(src, src).wait_recv()
        image = image + parts[1, src]

    curv_i[i] = pack4(dot(d, image, 1, 1))
    inner_send(curv_i, ci_send, ci_recv)
    rest = dot(jnp.concatenate([r, image], axis=0), image, 1, 1)
    sums_i[i] = pack4(rest)
    inner_send(sums_i, si_send, si_recv)
    gram = unpack4(blk_sum(grams_b, gb_send, gb_recv))
    unit = (lax.broadcasted_iota(jnp.int32, (rhs, rhs), 0) == lax.broadcasted_iota(jnp.int32, (rhs, rhs), 1)).astype(f32)
    inverse = eliminate(jnp.concatenate([gram, unit], axis=1), 0, rhs // 2)
    curv_b[b] = inner_sum(curv_i, ci_send, ci_recv)
    blk_send(curv_b, cb_send, cb_recv)
    sums_b[b] = inner_sum(sums_i, si_send, si_recv)
    blk_send(sums_b, sb_send, sb_recv)
    gram_inv = eliminate(inverse, rhs // 2, rhs)[:, rhs:]
    curv = unpack4(blk_sum(curv_b, cb_send, cb_recv))
    curv = 0.5 * (curv + curv.T)
    alpha = eliminate(jnp.concatenate([curv, gram], axis=1), 0, rhs)[:, rhs:]
    rest = unpack4(blk_sum(sums_b, sb_send, sb_recv))
    rq = rest[:rhs]
    alpha_t = alpha.T
    r_next = r - dot(alpha_t, image, 1, 0)
    moved = dot(rest, alpha, 1, 0)
    change = rq.T - moved[rhs:]
    inv_alpha = dot(gram_inv, alpha_t, 1, 0)
    beta = unit - dot(gram_inv, moved[:rhs], 1, 0) - dot(inv_alpha, change, 1, 0)
    res_out[...] = r_next
    sol_out[...] = sol[...] + dot(alpha_t, d, 1, 0)
    dir_out[...] = r_next + dot(beta.T, d, 1, 0)

    for off in range(1, ni):
        to = lax.rem(i + off, ni)
        w_copy(to, i).wait_send()
        p_copy(to, i).wait_send()
        s_copy(sums_i, i, to, i, si_send, si_recv, "inner").wait_send()
        s_copy(grams_i, i, to, i, gi_send, gi_recv, "inner").wait_send()
        s_copy(curv_i, i, to, i, ci_send, ci_recv, "inner").wait_send()

    @pl.loop(1, nb)
    def _(off):
        to = lax.rem(b + off, nb)
        s_copy(sums_b, b, to, b, sb_send, sb_recv, "blk").wait_send()
        s_copy(grams_b, b, to, b, gb_send, gb_recv, "blk").wait_send()
        s_copy(curv_b, b, to, b, cb_send, cb_recv, "blk").wait_send()
        c_copy(to, b).wait_send()


def write_out(a, b, c, a_out, b_out, c_out, sems):
    copies = [pltpu.make_async_copy(x, y, sems.at[k]) for k, (x, y) in enumerate(((a, a_out), (b, b_out), (c, c_out)))]
    for copy in copies:
        copy.start()
    for copy in copies:
        copy.wait()


def solution(mesh):
    nb, ni = mesh.shape["blk"], mesh.shape["inner"]

    def shards(points, inverse_scale, noise_var, sol, residual, direction):
        n, feats = points.shape
        rhs = direction.shape[1]
        dma = lambda k: pltpu.SemaphoreType.DMA((k,))
        vmem = pl.BlockSpec(memory_space=pltpu.VMEM)
        out = jax.ShapeDtypeStruct((rhs, n), f32)
        results = pl.pallas_call(
            functools.partial(kernel, nb, ni),
            out_shape=(out, out, out),
            in_specs=[pl.BlockSpec(memory_space=pltpu.HBM)] * 6,
            out_specs=(vmem, vmem, vmem),
            scratch_shapes=[
                pltpu.VMEM((feats, n), f32),
                pltpu.VMEM((1, feats), f32),
                pltpu.VMEM((1, n), f32),
                pltpu.VMEM((rhs, n), f32),
                pltpu.VMEM((rhs, n), f32),
                pltpu.VMEM((ni, feats, n), f32),
                pltpu.VMEM((nb, feats + rhs, n), f32),
                pltpu.VMEM((ni, n, 4 * feats), bf16),
                pltpu.VMEM((ni, n, 128), f32),
                pltpu.VMEM((4 * feats, n), bf16),
                pltpu.VMEM((1, n), f32),
                pltpu.VMEM((n, 128), bf16),
                pltpu.VMEM((ni, n, 128), f32),
                pltpu.VMEM((2, ni, rhs, n), f32),
                pltpu.VMEM((ni, rhs // 2, 4 * rhs), f32),
                pltpu.VMEM((nb, rhs // 2, 4 * rhs), f32),
                pltpu.VMEM((ni, rhs // 4, 4 * rhs), f32),
                pltpu.VMEM((nb, rhs // 4, 4 * rhs), f32),
                pltpu.VMEM((ni, rhs // 4, 4 * rhs), f32),
                pltpu.VMEM((nb, rhs // 4, 4 * rhs), f32),
                dma(6),
                dma(ni), dma(ni), dma(nb), dma(nb), dma(ni), dma(ni), dma(ni), dma(ni), dma(nb), dma(nb),
                dma(ni), dma(ni), dma(nb), dma(nb), dma(ni), dma(ni), dma(nb), dma(nb),
            ],
            compiler_params=pltpu.CompilerParams(
                collective_id=0, has_side_effects=True, vmem_limit_bytes=60 * 1024 * 1024),
        )(points.T, inverse_scale.reshape(1, feats), noise_var.reshape(1, n), sol.T, residual.T, direction.T)
        results = pl.pallas_call(
            write_out, out_shape=(out, out, out), in_specs=[vmem] * 3,
            out_specs=[pl.BlockSpec(memory_space=pltpu.HBM)] * 3, scratch_shapes=[dma(3)])(*results)
        return tuple(x.T for x in results)

    rows = P(("groups", "blk", "inner"), None)
    return jax.shard_map(
        shards, mesh=mesh,
        in_specs=(rows, P("groups"), P(("groups", "blk", "inner")), rows, rows, rows),
        out_specs=(rows, rows, rows), check_vma=False)
```

```python
import functools
import math

import jax
import jax.numpy as jnp
from jax import lax
from jax.experimental import pallas as pl
from jax.experimental.pallas import tpu as pltpu
from jax.sharding import PartitionSpec as P

MESH = pl.DeviceIdType.MESH
HIGH = lax.Precision.HIGHEST
LN2 = math.log(2.0)
FEATURE_SCALE = math.sqrt(5.0) / LN2
f32 = jnp.float32
bf16 = jnp.bfloat16


def dot(a, b, ca, cb, precision=HIGH):
    return lax.dot_general(a, b, (((ca,), (cb,)), ((), ())), precision=precision, preferred_element_type=f32)


def halves(x):
    hi = x.astype(bf16).astype(f32)
    lo = (x - hi).astype(bf16).astype(f32)
    return hi, lo


def row_operand(w):
    hi, lo = halves(w)
    both = jnp.concatenate([hi, lo], axis=0)
    norm = jnp.sum((hi + lo) * (hi + lo), axis=0, keepdims=True)
    both = (both.T * -2.0).astype(bf16)
    return jnp.concatenate([both, both], axis=1), jnp.broadcast_to(norm, (128, w.shape[1])).T


def col_operand(w):
    hi, lo = halves(w)
    norm = jnp.sum((hi + lo) * (hi + lo), axis=0, keepdims=True)
    hi, lo = hi.astype(bf16), lo.astype(bf16)
    return jnp.concatenate([hi, hi, lo, lo], axis=0), norm


def dir_operand(d):
    hi, lo = halves(d)
    return jnp.concatenate([hi, lo, jnp.zeros((64, d.shape[1]), f32)], axis=0).T.astype(bf16)


def eliminate(a, first, last):
    rows = lax.broadcasted_iota(jnp.int32, (a.shape[0], 1), 0)
    for k in range(first, last, 2):
        r0, r1 = a[k:k + 1, :], a[k + 1:k + 2, :]
        c0, c1 = a[:, k:k + 1], a[:, k + 1:k + 2]
        p01 = a[k:k + 1, k + 1:k + 2]
        inv0 = 1.0 / a[k:k + 1, k:k + 1]
        low = a[k + 1:k + 2, k:k + 1] * inv0
        inv1 = 1.0 / (a[k + 1:k + 2, k + 1:k + 2] - low * p01)
        r1 = (r1 - low * r0) * inv1
        r0 = (r0 - p01 * r1) * inv0
        a = jnp.where(rows == k, r0, jnp.where(rows == k + 1, r1, a - c0 * r0 - c1 * r1))
    return a


def pack4(x):
    n = x.shape[0] // 4
    return jnp.concatenate([x[g * n:(g + 1) * n] for g in range(4)], axis=1)


def unpack4(x):
    n = x.shape[1] // 4
    return jnp.concatenate([x[:, g * n:(g + 1) * n] for g in range(4)], axis=0)


def kernel(nb, ni, points_hbm, scale_hbm, noise_hbm, sol_hbm, res_hbm, dir_hbm, sol_out, res_out, dir_out,
           pts, scale, noise, sol, res, wrow, cols, a_op, rn, b_op, cn, d_op, acc, parts,
           sums_i, sums_b, grams_i, grams_b, curv_i, curv_b, l_sem,
           w_send, w_recv, c_send, c_recv, p_send, p_recv, si_send, si_recv, sb_send, sb_recv,
           gi_send, gi_recv, gb_send, gb_recv, ci_send, ci_recv, cb_send, cb_recv):
    feats, n = pts.shape
    rhs = sol.shape[0]
    b = lax.axis_index("blk")
    i = lax.axis_index("inner")

    local = [
        pltpu.make_async_copy(points_hbm, pts, l_sem.at[0]),
        pltpu.make_async_copy(scale_hbm, scale, l_sem.at[1]),
        pltpu.make_async_copy(dir_hbm, cols.at[b, feats:], l_sem.at[2]),
        pltpu.make_async_copy(res_hbm, res, l_sem.at[3]),
        pltpu.make_async_copy(noise_hbm, noise, l_sem.at[4]),
        pltpu.make_async_copy(sol_hbm, sol, l_sem.at[5]),
    ]
    for copy in local:
        copy.start()

    barrier = pltpu.get_barrier_semaphore()
    for off in range(1, ni):
        pl.semaphore_signal(barrier, inc=1, device_id={"inner": lax.rem(i + off, ni)}, device_id_type=MESH)

    @pl.loop(1, nb)
    def _(off):
        pl.semaphore_signal(barrier, inc=1, device_id={"blk": lax.rem(b + off, nb)}, device_id_type=MESH)

    for copy in local[:3]:
        copy.wait()
    same = lax.broadcasted_iota(jnp.int32, (feats, feats), 0) == lax.broadcasted_iota(jnp.int32, (feats, feats), 1)
    factor = jnp.sum(jnp.where(same, scale[...] * FEATURE_SCALE, 0.0), axis=1, keepdims=True)
    own_w = pts[...] * factor
    cols[b, :feats] = own_w
    pl.semaphore_wait(barrier, ni + nb - 2)

    def w_copy(to, src):
        return pltpu.make_async_remote_copy(
            src_ref=cols.at[b, :feats], dst_ref=wrow.at[src], send_sem=w_send.at[to], recv_sem=w_recv.at[src],
            device_id={"inner": to}, device_id_type=MESH)

    def c_copy(to, owner):
        return pltpu.make_async_remote_copy(
            src_ref=cols.at[owner], dst_ref=cols.at[owner], send_sem=c_send.at[to], recv_sem=c_recv.at[owner],
            device_id={"blk": to}, device_id_type=MESH)

    reach = jnp.minimum(b, nb - 1 - b)

    def owner_at(t):
        near = (t + 1) // 2
        paired = b + near * (1 - 2 * (t % 2))
        far = t - reach
        single = jnp.where(2 * b > nb - 1, b - far, b + far)
        return jnp.where(t <= 2 * reach, paired, single)

    @pl.loop(1, nb)
    def _(t):
        c_copy(owner_at(t), b).start()

    for off in range(1, ni):
        w_copy(lax.rem(i + off, ni), i).start()

    def s_copy(buf, me, to, src, send, recv, axis):
        return pltpu.make_async_remote_copy(
            src_ref=buf.at[me], dst_ref=buf.at[src], send_sem=send.at[to], recv_sem=recv.at[src],
            device_id={axis: to}, device_id_type=MESH)

    def inner_send(buf, send, recv):
        for off in range(1, ni):
            s_copy(buf, i, lax.rem(i + off, ni), i, send, recv, "inner").start()

    def inner_sum(buf, send, recv):
        for off in range(1, ni):
            src = lax.rem(i - off + ni, ni)
            s_copy(buf, i, src, src, send, recv, "inner").wait_recv()
        total = buf[0]
        for j in range(1, ni):
            total = total + buf[j]
        return total

    def blk_send(buf, send, recv):
        @pl.loop(1, nb)
        def _(off):
            s_copy(buf, b, lax.rem(b + off, nb), b, send, recv, "blk").start()

    def blk_sum(buf, send, recv):
        @pl.loop(1, nb)
        def _(off):
            src = lax.rem(b - off + nb, nb)
            s_copy(buf, b, src, src, send, recv, "blk").wait_recv()
        return lax.fori_loop(1, nb, lambda j, s: s + buf[j], buf[0])

    local[3].wait()
    r = res[...]
    grams_i[i] = pack4(dot(r, r, 1, 1))
    inner_send(grams_i, gi_send, gi_recv)
    acc[...] = jnp.zeros_like(acc)

    def prepare(j, w):
        op, norms = row_operand(w)
        a_op[j] = op
        rn[j] = norms

    def load_column(owner):
        op, norms = col_operand(cols[owner, :feats])
        b_op[...] = op
        cn[...] = norms
        d_op[...] = dir_operand(cols[owner, feats:])

    def tile(j):
        cross = dot(a_op[j], b_op[...], 1, 0, None)
        row_n = rn[j]
        x = cross + jnp.concatenate([row_n] * (n // 128), axis=1) + cn[...]
        x = jnp.maximum(x, 1e-30)
        v = x * lax.rsqrt(x)
        k = (1.0 + LN2 * v + (LN2 * LN2 / 3.0) * x) * jnp.exp2(-v)
        kh = k.astype(bf16)
        kl = (k - kh.astype(f32)).astype(bf16)
        return acc[j] + dot(kh, d_op[...], 1, 0, None) + dot(kl, d_op[...], 1, 0, None)

    prepare(i, own_w)
    load_column(b)

    @pl.loop(0, ni)
    def _(off):
        j = lax.rem(i - off + ni, ni)

        @pl.when(off > 0)
        def _():
            w_copy(j, j).wait_recv()
            prepare(j, wrow[j])

        acc[j] = tile(j)

    grams_b[b] = inner_sum(grams_i, gi_send, gi_recv)
    blk_send(grams_b, gb_send, gb_recv)

    def receive(t):
        owner = owner_at(t)
        c_copy(owner, owner).wait_recv()
        load_column(owner)

    @pl.loop(1, nb - 1)
    def _(t):
        receive(t)

        @pl.loop(0, ni, unroll=ni)
        def _(j):
            acc[j] = tile(j)


    receive(nb - 1)

    def p_copy(to, src):
        return pltpu.make_async_remote_copy(
            src_ref=parts.at[0, to], dst_ref=parts.at[1, src], send_sem=p_send.at[to], recv_sem=p_recv.at[src],
            device_id={"inner": to}, device_id_type=MESH)

    def finished(j):
        a = tile(j).T
        return a[:rhs] + a[rhs:2 * rhs]

    @pl.loop(1, ni, unroll=ni - 1)
    def _(off):
        to = lax.rem(i + off, ni)
        parts[0, to] = finished(to)
        p_copy(to, i).start()

    local[4].wait()
    local[5].wait()
    d = cols[b, feats:]
    image = finished(i) + noise[...] * d
    for off in range(1, ni):
        src = lax.rem(i - off + ni, ni)
        p_copy(src, src).wait_recv()
        image = image + parts[1, src]

    curv_i[i] = pack4(dot(d, image, 1, 1))
    inner_send(curv_i, ci_send, ci_recv)
    rest = dot(jnp.concatenate([r, image], axis=0), image, 1, 1)
    sums_i[i] = pack4(rest)
    inner_send(sums_i, si_send, si_recv)
    gram = unpack4(blk_sum(grams_b, gb_send, gb_recv))
    unit = (lax.broadcasted_iota(jnp.int32, (rhs, rhs), 0) == lax.broadcasted_iota(jnp.int32, (rhs, rhs), 1)).astype(f32)
    inverse = eliminate(jnp.concatenate([gram, unit], axis=1), 0, rhs // 2)
    curv_b[b] = inner_sum(curv_i, ci_send, ci_recv)
    blk_send(curv_b, cb_send, cb_recv)
    sums_b[b] = inner_sum(sums_i, si_send, si_recv)
    blk_send(sums_b, sb_send, sb_recv)
    gram_inv = eliminate(inverse, rhs // 2, rhs)[:, rhs:]
    curv = unpack4(blk_sum(curv_b, cb_send, cb_recv))
    curv = 0.5 * (curv + curv.T)
    alpha = eliminate(jnp.concatenate([curv, gram], axis=1), 0, rhs)[:, rhs:]
    rest = unpack4(blk_sum(sums_b, sb_send, sb_recv))
    rq = rest[:rhs]
    alpha_t = alpha.T
    r_next = r - dot(alpha_t, image, 1, 0)
    moved = dot(rest, alpha, 1, 0)
    change = rq.T - moved[rhs:]
    inv_alpha = dot(gram_inv, alpha_t, 1, 0)
    beta = unit - dot(gram_inv, moved[:rhs], 1, 0) - dot(inv_alpha, change, 1, 0)
    res_out[...] = r_next
    sol_out[...] = sol[...] + dot(alpha_t, d, 1, 0)
    dir_out[...] = r_next + dot(beta.T, d, 1, 0)

    for off in range(1, ni):
        to = lax.rem(i + off, ni)
        w_copy(to, i).wait_send()
        p_copy(to, i).wait_send()
        s_copy(sums_i, i, to, i, si_send, si_recv, "inner").wait_send()
        s_copy(grams_i, i, to, i, gi_send, gi_recv, "inner").wait_send()
        s_copy(curv_i, i, to, i, ci_send, ci_recv, "inner").wait_send()

    @pl.loop(1, nb)
    def _(off):
        to = lax.rem(b + off, nb)
        s_copy(sums_b, b, to, b, sb_send, sb_recv, "blk").wait_send()
        s_copy(grams_b, b, to, b, gb_send, gb_recv, "blk").wait_send()
        s_copy(curv_b, b, to, b, cb_send, cb_recv, "blk").wait_send()
        c_copy(to, b).wait_send()


def write_out(a, b, c, a_out, b_out, c_out, sems):
    copies = [pltpu.make_async_copy(x, y, sems.at[k]) for k, (x, y) in enumerate(((a, a_out), (b, b_out), (c, c_out)))]
    for copy in copies:
        copy.start()
    for copy in copies:
        copy.wait()


def solution(mesh):
    nb, ni = mesh.shape["blk"], mesh.shape["inner"]

    def shards(points, inverse_scale, noise_var, sol, residual, direction):
        n, feats = points.shape
        rhs = direction.shape[1]
        dma = lambda k: pltpu.SemaphoreType.DMA((k,))
        vmem = pl.BlockSpec(memory_space=pltpu.VMEM)
        out = jax.ShapeDtypeStruct((rhs, n), f32)
        results = pl.pallas_call(
            functools.partial(kernel, nb, ni),
            out_shape=(out, out, out),
            in_specs=[pl.BlockSpec(memory_space=pltpu.HBM)] * 6,
            out_specs=(vmem, vmem, vmem),
            scratch_shapes=[
                pltpu.VMEM((feats, n), f32),
                pltpu.VMEM((1, feats), f32),
                pltpu.VMEM((1, n), f32),
                pltpu.VMEM((rhs, n), f32),
                pltpu.VMEM((rhs, n), f32),
                pltpu.VMEM((ni, feats, n), f32),
                pltpu.VMEM((nb, feats + rhs, n), f32),
                pltpu.VMEM((ni, n, 4 * feats), bf16),
                pltpu.VMEM((ni, n, 128), f32),
                pltpu.VMEM((4 * feats, n), bf16),
                pltpu.VMEM((1, n), f32),
                pltpu.VMEM((n, 128), bf16),
                pltpu.VMEM((ni, n, 128), f32),
                pltpu.VMEM((2, ni, rhs, n), f32),
                pltpu.VMEM((ni, rhs // 2, 4 * rhs), f32),
                pltpu.VMEM((nb, rhs // 2, 4 * rhs), f32),
                pltpu.VMEM((ni, rhs // 4, 4 * rhs), f32),
                pltpu.VMEM((nb, rhs // 4, 4 * rhs), f32),
                pltpu.VMEM((ni, rhs // 4, 4 * rhs), f32),
                pltpu.VMEM((nb, rhs // 4, 4 * rhs), f32),
                dma(6),
                dma(ni), dma(ni), dma(nb), dma(nb), dma(ni), dma(ni), dma(ni), dma(ni), dma(nb), dma(nb),
                dma(ni), dma(ni), dma(nb), dma(nb), dma(ni), dma(ni), dma(nb), dma(nb),
            ],
            compiler_params=pltpu.CompilerParams(
                collective_id=0, has_side_effects=True, vmem_limit_bytes=60 * 1024 * 1024),
        )(points.T, inverse_scale.reshape(1, feats), noise_var.reshape(1, n), sol.T, residual.T, direction.T)
        results = pl.pallas_call(
            write_out, out_shape=(out, out, out), in_specs=[vmem] * 3,
            out_specs=[pl.BlockSpec(memory_space=pltpu.HBM)] * 3, scratch_shapes=[dma(3)])(*results)
        return tuple(x.T for x in results)

    rows = P(("groups", "blk", "inner"), None)
    return jax.shard_map(
        shards, mesh=mesh,
        in_specs=(rows, P("groups"), P(("groups", "blk", "inner")), rows, rows, rows),
        out_specs=(rows, rows, rows), check_vma=False)
```
